32 devices in a mesh: group: 2 (over y), head: 4 (over z), req: 2 (over x), pd: 2 (over core).
Axes of the slice: x: 2, y: 2, z: 4, core: 2. Of those that a mesh axis runs over, the one named last changes fastest.
Arguments:
- x_pre: bfloat16 [32, 512, 128, 128], P(('group', 'req', 'pd'), None, 'head'), parts along dimension 0, may hold values from -6 to 6
- dt_pre: float32 [32, 512, 128], P(('group', 'req', 'pd'), None, 'head'), parts along dimension 0, may hold values from 0.002 to 0.5
- b_pre: bfloat16 [32, 512, 8, 128], P(('group', 'req', 'pd')), parts along dimension 0, may hold values from -0.5 to 0.5
- c_pre: bfloat16 [32, 512, 8, 128], P(('group', 'req', 'pd')), parts along dimension 0, may hold values from -6 to 6
- rate: float32 [128], replicated, may hold values from 0.01 to 4
- skip: float32 [128], replicated, may hold values from 0.2 to 1.5
- lengths: int32 [32], P('group'), parts along dimension 0, may hold values from 1 to 512, 4096 in all
- table: int32 [32, 16], P('group'), parts along dimension 0, may hold values from 0 to 15, each once within a row
- kv_pages: bfloat16 [32, 8, 16, 2, 32, 128], P(('group', 'req', 'pd'), None, 'head'), parts along dimension 0, may hold values from -6 to 6
- query: bfloat16 [32, 4, 8, 1024], P(('group', 'head'), None, ('req', 'pd')), parts along dimension 0, may hold values from -6 to 6
- kv_new: bfloat16 [32, 4, 8, 2, 128], P(('group', 'head'), None, ('req', 'pd')), parts along dimension 0, may hold values from -6 to 6
- x_dec: bfloat16 [32, 4, 4, 32, 128], P(('group', 'head'), None, None, ('req', 'pd')), parts along dimension 0, may hold values from -6 to 6
- dt_dec: float32 [32, 4, 4, 32], P(('group', 'head'), None, None, ('req', 'pd')), parts along dimension 0, may hold values from 0.002 to 0.5
- b_dec: bfloat16 [32, 4, 8, 128], P(('group', 'head')), parts along dimension 0, may hold values from -0.5 to 0.5
- c_dec: bfloat16 [32, 4, 8, 128], P(('group', 'head')), parts along dimension 0, may hold values from -6 to 6
Outputs:
- prefill_out: bfloat16 [32, 512, 128, 128], P(('group', 'req', 'pd'), None, 'head'), parts along dimension 0
- decode_out: bfloat16 [32, 4, 4, 32, 128], P(('group', 'head'), None, None, ('req', 'pd')), parts along dimension 0
- decode_state: float32 [32, 4, 32, 128, 128], P(('group', 'head'), None, ('req', 'pd')), parts along dimension 0
- attn_out: bfloat16 [32, 4, 8, 1024], P(('group', 'head'), None, ('req', 'pd')), parts along dimension 0
The draws below stay inside these ranges and needn't reach their ends.
There are 2 independent parts, one for each index of `group`. The reference program is written for one: setup_inputs(seed, part) draws one part's arguments, and reference() takes and returns one part's arrays. A program takes and returns all parts, laid end to end along the dimension named above; an argument that names none is the same for every part. Nothing has to cross between parts.
Inputs may be any that keep to these rules, and one draw needn't show every extreme that they name: `lengths`: the longest span has exactly 512 valid tokens. `table`: each row is a permutation.
All inputs are finite; a program needn't handle non-finite values.
Results may differ from the reference program's by a relative error of at most 0.001.
Values may be sent and summed in bfloat16 or wider, within the bound.
No kernel may reach another device: no remote copies, remote signals or barrier semaphores. Data moves between devices by JAX's collectives and lax.ppermute only.
A program may use at most 256 MiB of HBM per device.

```python
import math
import jax
import jax.numpy as jnp
import numpy as np
from jax import lax

H = 128
P_SIZE = 128
N = 128
G = 8
KVH = 8
HEAD_SIZE = 128
SPAN = 512
BLOCK = 128
PAGE_TOKENS = 32
STEPS = 4
GQ = 8
PAGES = 16
REQS = 16
N_HEAD = 4


def draw_x_pre(key, part):
    key = jax.random.fold_in(key, 11)
    key_base, key_pick, key_shift, key_coin = jax.random.split(key, 4)
    base_values = jnp.clip(jax.random.normal(key_base, (REQS, SPAN, H, P_SIZE), jnp.float32), -6.0, 6.0)
    quiet_request = jax.random.randint(key_pick, (REQS,), 0, 4) == 0
    offsets = jax.random.randint(key_shift, (REQS,), 0, BLOCK)
    positions = jnp.arange(SPAN, dtype=jnp.int32)
    windows = (positions[None, :] + offsets[:, None]) // BLOCK
    coin_flips = jax.random.randint(key_coin, (REQS, SPAN // BLOCK + 1), 0, 2)
    quiet_mask = quiet_request[:, None] & (jnp.take_along_axis(coin_flips, windows, axis=1) == 1)
    factor = jnp.where(quiet_mask, jnp.float32(0.001), jnp.float32(1.0))
    return (base_values * factor[:, :, None, None]).astype(jnp.bfloat16)


def draw_dt_pre(key, part):
    key = jax.random.fold_in(key, 12)
    key_pick, key_unit = jax.random.split(key, 2)
    slow_pair = jax.random.randint(key_pick, (REQS, 1, H), 0, 4) == 0
    unit_draw = jax.random.uniform(key_unit, (REQS, SPAN, H), jnp.float32)
    wide_values = jnp.exp(jnp.log(0.002) + unit_draw * jnp.log(250.0))
    narrow_values = jnp.exp(jnp.log(0.002) + unit_draw * jnp.log(5.0))
    values = jnp.where(slow_pair, narrow_values, wide_values)
    return jnp.clip(values, 0.002, 0.5).astype(jnp.float32)


def draw_rate(key, part):
    key = jax.random.fold_in(key, 13)
    key_pick, key_unit = jax.random.split(key, 2)
    fast_heads = jax.random.randint(key_pick, (H,), 0, 2) == 1
    unit_draw = jax.random.uniform(key_unit, (H,), jnp.float32)
    fast_values = jnp.exp(jnp.log(0.5) + unit_draw * jnp.log(8.0))
    slow_values = jnp.exp(jnp.log(0.01) + unit_draw * jnp.log(50.0))
    values = jnp.where(fast_heads, fast_values, slow_values)
    return jnp.clip(values, 0.01, 4.0).astype(jnp.float32)


def levels(key, shape, cuts, low, top_value):
    def one(position, parts):
        steps = jax.random.uniform(jax.random.fold_in(jax.random.fold_in(key, 6), position), (parts,), jnp.float32, low / len(cuts), top_value / len(cuts))
        return jnp.repeat(jnp.exp(steps), shape[position] // parts).reshape((-1,) + (1,) * (len(shape) - position - 1))

    gain = one(*cuts[0])
    for cut in cuts[1:]:
        gain = gain * one(*cut)
    return gain


def profile(count, total, limit, slope):
    weights = [(1 << 20) // math.isqrt(grade ** slope) + 1 for grade in range(2, count + 1)]
    surplus, given = total - limit - (count - 1), [1] * (count - 1)
    while surplus > 0:
        free = [i for i in range(count - 1) if given[i] < limit]
        pool, left = sum([weights[i] for i in free]), surplus
        for i in free:
            extra = min(limit - given[i], max(1, left * weights[i] // pool), surplus)
            given[i] = given[i] + extra
            surplus = surplus - extra
    return np.array([limit] + given)


def uneven(own_key, count, total, bound, lean):
    if count == 2:
        one = jax.random.randint(own_key, (), max(1, total - bound), min(bound, total - 1) + 1)
        return jnp.stack([one, total - one])
    tallies = jnp.asarray(profile(count, total, bound, lean), jnp.int32)
    pairs = (count - 1) // 2
    giver, receiver = tallies[1:1 + 2 * pairs:2], tallies[2:2 + 2 * pairs:2]
    room = jnp.minimum(giver - 1, bound - receiver)
    passed = jax.random.randint(jax.random.fold_in(own_key, 1), (pairs,), 0, 1 << 20) % (room + 1)
    tallies = tallies.at[1:1 + 2 * pairs:2].set(giver - passed).at[2:2 + 2 * pairs:2].set(receiver + passed)
    return tallies[jax.random.permutation(jax.random.fold_in(own_key, 2), count)]


def noise(stream_key, dims, spread, most, cuts=(), held_as=jnp.bfloat16):
    entries = spread * jax.random.normal(stream_key, dims, jnp.float32)
    if cuts:
        entries = entries * levels(stream_key, dims, cuts, -0.22, 0.18)
    return jnp.clip(entries, -most, most).astype(held_as)


def setup_inputs(seed: int = 0, part: int = 0) -> dict:
    key_of = jax.random.split(jax.random.key(seed), 16)
    part_keys = jax.random.split(jax.random.fold_in(key_of[15], part), 16)
    x_pre = draw_x_pre(jax.random.fold_in(jax.random.fold_in(key_of[15], part), 71), part)
    dt_pre = draw_dt_pre(jax.random.fold_in(jax.random.fold_in(key_of[15], part), 71), part)
    b_pre = noise(part_keys[2], (REQS, SPAN, G, N), N ** -0.5, 0.5, ((0, 4),))
    c_pre = noise(part_keys[3], (REQS, SPAN, G, N), 1.0, 6.0, ((0, 4),))
    rate = draw_rate(jax.random.fold_in(key_of[15], 71), part)
    skip = jnp.clip(jax.random.uniform(key_of[5], (H,), jnp.float32, 0.2, 1.5), 0.2, 1.5)
    lengths = uneven(part_keys[6], REQS, REQS * SPAN // 2, SPAN, 2).astype(jnp.int32)
    table = jax.vmap(lambda own: jax.random.permutation(own, PAGES))(jax.random.split(part_keys[7], REQS)).reshape((REQS, PAGES)).astype(jnp.int32)
    kv_pages = noise(part_keys[8], (REQS, KVH, PAGES, 2, PAGE_TOKENS, HEAD_SIZE), 1.0, 6.0, ((0, 4), (2, 4)))
    query = noise(part_keys[9], (REQS, STEPS, KVH, GQ * HEAD_SIZE), 1.0, 6.0, ((0, 4), (2, 4)))
    kv_new = noise(part_keys[10], (REQS, STEPS, KVH, 2, HEAD_SIZE), 1.0, 6.0, ((0, 4), (2, 4)))
    x_dec = noise(part_keys[11], (REQS, STEPS, N_HEAD, H // N_HEAD, P_SIZE), 1.0, 6.0, ((0, 4), (3, 4)))
    dt_dec = jnp.clip(jnp.exp(math.log(0.5) - 5.521461 * jax.random.uniform(part_keys[12], (REQS, STEPS, N_HEAD, H // N_HEAD), jnp.float32) ** levels(part_keys[12], (REQS, STEPS, N_HEAD, H // N_HEAD), ((0, 4), (3, 4)), -0.2, 0.2)), 0.002, 0.5)
    b_dec = noise(part_keys[13], (REQS, STEPS, G, N), N ** -0.5, 0.5, ((0, 4),))
    c_dec = noise(part_keys[14], (REQS, STEPS, G, N), 1.0, 6.0, ((0, 4),))
    return {"x_pre": x_pre, "dt_pre": dt_pre, "b_pre": b_pre, "c_pre": c_pre, "rate": rate, "skip": skip, "lengths": lengths, "table": table, "kv_pages": kv_pages, "query": query, "kv_new": kv_new, "x_dec": x_dec, "dt_dec": dt_dec, "b_dec": b_dec, "c_dec": c_dec}


HIGH = lax.Precision.HIGHEST


def span_scan(x, bh, ch, dt, rate, skip, length):
    request_count, tlen, heads, hsize = x.shape
    nstate = bh.shape[-1]
    nblk = tlen // BLOCK
    valid = jnp.arange(tlen, dtype=jnp.int32)[None, :] < length[:, None]
    dtm = jnp.where(valid[:, :, None], dt, jnp.float32(0.0))

    def blocks(arr):
        return jnp.swapaxes(arr.reshape((request_count, nblk, BLOCK) + arr.shape[2:]), 0, 1)

    tri = jnp.arange(BLOCK)[:, None] >= jnp.arange(BLOCK)[None, :]

    def step(state, blk):
        xs, bs, cs, ds = blk
        xf = xs.astype(jnp.float32)
        bf = bs.astype(jnp.float32)
        cf = cs.astype(jnp.float32)
        cum = jnp.cumsum(-rate[None, None, :] * ds, axis=1)
        diff = cum[:, :, None, :] - cum[:, None, :, :]
        mask = tri[None, :, :, None]
        seg = jnp.where(mask, jnp.exp(jnp.where(mask, diff, jnp.float32(0.0))), jnp.float32(0.0))
        scores = jnp.einsum('rthn,ruhn->rtuh', cf, bf, precision=HIGH)
        weights = seg * scores * ds[:, None, :, :]
        out = jnp.einsum('rtuh,ruhp->rthp', weights, xf, precision=HIGH)
        out = out + jnp.exp(cum)[..., None] * jnp.einsum('rthn,rhpn->rthp', cf, state, precision=HIGH)
        out = out + skip[None, None, :, None] * xf
        tail = jnp.exp(cum[:, -1:, :] - cum) * ds
        state = jnp.exp(cum[:, -1, :])[:, :, None, None] * state + jnp.einsum('ruh,ruhp,ruhn->rhpn', tail, xf, bf, precision=HIGH)
        return state, out

    start = jnp.zeros((request_count, heads, hsize, nstate), jnp.float32)
    final, outs = lax.scan(step, start, (blocks(x), blocks(bh), blocks(ch), blocks(dtm)))
    outs = jnp.swapaxes(outs, 0, 1).reshape(request_count, tlen, heads, hsize)
    outs = jnp.where(valid[:, :, None, None], outs, jnp.float32(0.0))
    return outs.astype(jnp.bfloat16), final


def decode_steps(state, x, bh, ch, dt, rate, skip):
    outs = []
    for step in range(x.shape[1]):
        xf = x[:, step].astype(jnp.float32)
        decay = jnp.exp(-rate[None, :] * dt[:, step])
        state = decay[:, :, None, None] * state + (dt[:, step][:, :, None, None] * xf[:, :, :, None]) * bh[:, step].astype(jnp.float32)[:, :, None, :]
        out = jnp.einsum('rhn,rhpn->rhp', ch[:, step].astype(jnp.float32), state, precision=HIGH) + skip[None, :, None] * xf
        outs.append(out.astype(jnp.bfloat16))
    return jnp.stack(outs, axis=1), state


def reference(x_pre, dt_pre, b_pre, c_pre, rate, skip, lengths, table, kv_pages, query, kv_new, x_dec, dt_dec, b_dec, c_dec):
    groups = jnp.arange(H, dtype=jnp.int32) // (H // G)

    def one(items):
        xs, ds, bs, cs, ln = items
        outs, final = span_scan(xs[None], bs[:, groups][None], cs[:, groups][None], ds[None], rate, skip, ln[None])
        return outs[0], final[0]

    prefill_out, states = lax.map(one, (x_pre, dt_pre, b_pre, c_pre, lengths))
    xd = x_dec.reshape(REQS, STEPS, H, P_SIZE)
    dtd = dt_dec.reshape(REQS, STEPS, H)
    dec_out, dec_state = decode_steps(states, xd, b_dec[:, :, groups], c_dec[:, :, groups], dtd, rate, skip)
    decode_out = dec_out.reshape(REQS, STEPS, N_HEAD, H // N_HEAD, P_SIZE)
    decode_state = dec_state.reshape(REQS, N_HEAD, H // N_HEAD, P_SIZE, N)

    scale = 1.0 / (HEAD_SIZE ** 0.5)
    key_rows = kv_pages[:, :, :, 0].reshape(REQS, KVH, PAGES * PAGE_TOKENS, HEAD_SIZE).astype(jnp.float32)
    value_rows = kv_pages[:, :, :, 1].reshape(REQS, KVH, PAGES * PAGE_TOKENS, HEAD_SIZE).astype(jnp.float32)
    positions = (table[:, :, None] * PAGE_TOKENS + jnp.arange(PAGE_TOKENS, dtype=jnp.int32)[None, None, :]).reshape(REQS, PAGES * PAGE_TOKENS)
    valid = positions < lengths[:, None]
    qf = query.reshape(REQS, STEPS, KVH, GQ, HEAD_SIZE).astype(jnp.float32)
    s_cache = jnp.einsum('rskgd,rkjd->rskgj', qf, key_rows, precision=HIGH) * scale
    s_cache = jnp.where(valid[:, None, None, None, :], s_cache, -jnp.inf)
    new_keys = kv_new[:, :, :, 0].astype(jnp.float32)
    new_vals = kv_new[:, :, :, 1].astype(jnp.float32)
    s_new = jnp.einsum('rskgd,rukd->rskgu', qf, new_keys, precision=HIGH) * scale
    causal = jnp.arange(STEPS)[:, None] >= jnp.arange(STEPS)[None, :]
    s_new = jnp.where(causal[None, :, None, None, :], s_new, -jnp.inf)
    top = jnp.maximum(jnp.max(s_cache, axis=-1), jnp.max(s_new, axis=-1))
    p_cache = jnp.exp(s_cache - top[..., None])
    p_new = jnp.exp(s_new - top[..., None])
    total = jnp.sum(p_cache, axis=-1) + jnp.sum(p_new, axis=-1)
    acc = jnp.einsum('rskgj,rkjd->rskgd', p_cache, value_rows, precision=HIGH) + jnp.einsum('rskgu,rukd->rskgd', p_new, new_vals, precision=HIGH)
    attn_out = (acc / total[..., None]).reshape(REQS, STEPS, KVH, GQ * HEAD_SIZE).astype(jnp.bfloat16)
    return prefill_out, decode_out, decode_state, attn_out
```

```python
import functools

import jax
import jax.numpy as jnp
from jax import lax
from jax.experimental import pallas as pl
from jax.experimental.pallas import tpu as pltpu
from jax.sharding import PartitionSpec as P

H = 128
G = 8
HEAD_SIZE = 128
BLOCK = 128
PAGE_TOKENS = 32
NEG = -1e30
F32 = jnp.float32
BF16 = jnp.bfloat16
AXES = ("head", "req", "pd")
CODE = 240.0
PAD_ROWS = 16


def dot(a, b):
    return jnp.dot(a, b, preferred_element_type=F32)


def dot_nt(a, b):
    return lax.dot_general(a, b, (((1,), (1,)), ((), ())), preferred_element_type=F32)


def split2(v):
    high = v.astype(BF16)
    return high, (v - high.astype(F32)).astype(BF16)


def split3(v):
    high = v.astype(BF16)
    rest = v - high.astype(F32)
    middle = rest.astype(BF16)
    return high, middle, (rest - middle.astype(F32)).astype(BF16)


def swap_matrix(rows, cols):
    n = rows * cols
    i = lax.broadcasted_iota(jnp.int32, (n, n), 0)
    j = lax.broadcasted_iota(jnp.int32, (n, n), 1)
    return ((i // rows == j % cols) & (i % rows == j // cols)).astype(F32).astype(BF16)


def token_mask(shape, dim, length, start=0):
    return lax.broadcasted_iota(jnp.int32, shape, dim) + start < length


def state_kernel(sc, x_ref, dt_ref, rate_ref, bt_ref, out_ref, perm, tri, xs, *, hb, part, first):
    r = pl.program_id(0)
    head, block, flip = sc[0], sc[1], sc[2]
    length = sc[4 + first + r]
    span = x_ref.shape[1]
    heads = dt_ref.shape[2]

    @pl.when(r == 0)
    def _():
        perm[...] = swap_matrix(16, hb)
        i = lax.broadcasted_iota(jnp.int32, (span, span), 0)
        j = lax.broadcasted_iota(jnp.int32, (span, span), 1)
        tri[...] = (i > j).astype(F32).astype(BF16)

    dtm = jnp.where(token_mask((span, heads), 0, length), dt_ref[0], 0.0)
    decay = -rate_ref[pl.ds(head, 1), :] * dtm
    decay_t, dtm_t = decay.T, dtm.T
    after = sum(dot(p, tri[...]) for p in split3(decay_t)[::-1])
    tails = jnp.exp(after) * dtm_t
    tail = tails[0:hb]
    for k in range(1, heads // hb):
        tail = jnp.where(block == k, tails[k * hb : (k + 1) * hb], tail)
    for k in range(span // BLOCK):
        lo = k * BLOCK

        @pl.when(lo < length)
        def _():
            for t in range(lo, lo + BLOCK, 16):
                y = dot(perm[...], x_ref[0, t : t + 16].reshape(16 * hb, 128)).astype(BF16)
                for h in range(hb):
                    xs[h, t : t + 16, :] = y[h * 16 : (h + 1) * 16]

        @pl.when(lo >= length)
        def _():
            xs[:, lo : lo + BLOCK, :] = jnp.zeros((hb, BLOCK, 128), BF16)

    bt = bt_ref[0, 0].astype(F32)
    for h in range(hb):
        high, low = split2(bt * tail[h : h + 1])
        st = dot(high, xs[h]) + dot(low, xs[h])
        top = (jnp.max(jnp.abs(st), axis=0, keepdims=True) * 1.01 + 1e-30).astype(BF16)
        level = jnp.abs(st) * (CODE / top.astype(F32)) - CODE / 2
        code = jnp.exp2(level)
        code = jnp.where(st < 0, -code, code).astype(BF16)
        p, local = h // part, h % part
        slot = jnp.bitwise_xor(p, flip)
        out_ref[0, slot, local * 128 : (local + 1) * 128, :] = code
        if local == 0:
            tops = []
        tops.append(top.astype(F32))
        if local == part - 1:
            tops.append(jnp.zeros((PAD_ROWS - part, 128), F32))
            out_ref[0, slot, part * 128 :, :] = jnp.concatenate(tops, axis=0).astype(BF16)


def span_states(sc, x, dt, rate2, bt, hb, part, first, count):
    _, span, heads, width = x.shape
    slots = hb // part
    rows = part * 128 + PAD_ROWS
    return pl.pallas_call(
        functools.partial(state_kernel, hb=hb, part=part, first=first),
        grid_spec=pltpu.PrefetchScalarGridSpec(
            num_scalar_prefetch=1,
            grid=(count,),
            in_specs=[
                pl.BlockSpec((1, span, hb, width), lambda r, s: (r + first, 0, s[1], 0)),
                pl.BlockSpec((1, span, heads), lambda r, s: (r + first, 0, 0)),
                pl.BlockSpec(rate2.shape, lambda r, s: (0, 0)),
                pl.BlockSpec((1, 1, 128, span), lambda r, s: (r + first, s[1], 0, 0)),
            ],
            out_specs=pl.BlockSpec((1, slots, rows, 128), lambda r, s: (r, 0, 0, 0)),
            scratch_shapes=[
                pltpu.VMEM((16 * hb, 16 * hb), BF16),
                pltpu.VMEM((span, span), BF16),
                pltpu.VMEM((hb, span, 128), BF16),
            ],
        ),
        out_shape=jax.ShapeDtypeStruct((count, slots, rows, 128), BF16),
        compiler_params=pltpu.CompilerParams(vmem_limit_bytes=40 << 20),
        cost_estimate=pl.CostEstimate(
            flops=count * hb * 4 * span * 128 * 128,
            bytes_accessed=count * hb * (span + 128) * 256,
            transcendentals=count * hb * 128 * 128,
        ),
        name="span_states",
    )(sc, x, dt, rate2, bt)


def scan_kernel(sc, x_ref, dt_ref, rate_ref, skip_ref, bt_ref, c_ref, out_ref, perm, back, tri, xs, os, state, cols, *, hb, first):
    r = pl.program_id(0)
    block = pl.program_id(1)
    head = sc[0]
    length = sc[4 + first + r]
    span = x_ref.shape[1]
    heads = dt_ref.shape[2]
    count = span // BLOCK

    @pl.when((r == 0) & (block == 0))
    def _():
        perm[...] = swap_matrix(16, hb)
        back[...] = swap_matrix(hb, 16)
        i = lax.broadcasted_iota(jnp.int32, (BLOCK, BLOCK), 0)
        j = lax.broadcasted_iota(jnp.int32, (BLOCK, BLOCK), 1)
        tri[...] = (i >= j).astype(F32).astype(BF16)

    causal = tri[...].astype(F32)
    rates = -rate_ref[pl.ds(head, 1), :]
    skips = skip_ref[pl.ds(head, 1), :]

    def pick(v):
        out = v[:, 0:hb]
        for k in range(1, heads // hb):
            out = jnp.where(block == k, v[:, k * hb : (k + 1) * hb], out)
        return out

    skips = pick(skips)
    for k in range(count):
        lo = k * BLOCK

        @pl.when(lo >= length)
        def _():
            out_ref[0, lo : lo + BLOCK] = jnp.zeros((BLOCK, hb, 128), BF16)

        @pl.when(lo < length)
        def _():
            valid = token_mask((BLOCK, hb), 0, length, lo)
            dt = pick(dt_ref[0, lo : lo + BLOCK])
            dtm = jnp.where(valid, dt, 0.0)
            cum = sum(dot(tri[...], p) for p in split3(pick(rates) * dtm)[::-1])
            level = cum - jnp.where(valid, jnp.log(dt), NEG)
            level_t = level.T
            scores = dot(c_ref[0, 0, lo : lo + BLOCK], bt_ref[0, 0, :, lo : lo + BLOCK]) * causal
            c = c_ref[0, 0, lo : lo + BLOCK]
            cc = jnp.concatenate([c, c], axis=1)
            grown = jnp.exp(cum)
            last = cum[BLOCK - 1 : BLOCK, :]
            last_t = jnp.exp(last)
            bt = bt_ref[0, 0, :, lo : lo + BLOCK].astype(F32)
            total_t = cum.T[:, BLOCK - 1 : BLOCK]
            tail = jnp.exp(total_t - level_t)
            keep = token_mask((BLOCK, 128), 0, length, lo)
            for t in range(0, BLOCK, 16):
                y = dot(perm[...], x_ref[0, lo + t : lo + t + 16].reshape(16 * hb, 128)).astype(BF16)
                for h in range(hb):
                    xs[h, t : t + 16, :] = y[h * 16 : (h + 1) * 16]
            for h in range(hb):
                diff = cum[:, h : h + 1] - level_t[h : h + 1, :]
                weights = jnp.exp(jnp.minimum(diff, 80.0)) * scores
                left = jnp.concatenate(split2(weights), axis=1)
                x = xs[h]
                if k < count - 1:
                    left = jnp.concatenate(
                        [left, jnp.concatenate(split2(bt * tail[h : h + 1]), axis=1)], axis=0
                    )
                both = dot(left, jnp.concatenate([x, x], axis=0))
                out = both[:BLOCK] + skips[:, h : h + 1] * x.astype(F32)
                if k > 0:
                    old = state[h]
                    inter = dot(cc, jnp.concatenate(split2(old), axis=0))
                    out = out + grown[:, h : h + 1] * inter
                if k < count - 1:
                    new = both[BLOCK:]
                    if k > 0:
                        new = new + last_t[:, h : h + 1] * old
                    state[h] = new
                os[h] = jnp.where(keep, out, 0.0).astype(BF16)
            for t in range(0, BLOCK, 16):
                y = dot(back[...], os[:, t : t + 16, :].reshape(hb * 16, 128)).astype(BF16)
                out_ref[0, lo + t : lo + t + 16] = y.reshape(16, hb, 128)


def span_scan(sc, x, dt, rate2, skip2, bt, c, hb, first, count, out):
    reqs, span, heads, width = x.shape
    blocks = heads // hb
    x_spec = pl.BlockSpec((1, span, hb, width), lambda r, b, s: (r + first, 0, b, 0))
    in_specs = [
        x_spec,
        pl.BlockSpec((1, span, heads), lambda r, b, s: (r + first, 0, 0)),
        pl.BlockSpec(rate2.shape, lambda r, b, s: (0, 0)),
        pl.BlockSpec(skip2.shape, lambda r, b, s: (0, 0)),
        pl.BlockSpec((1, 1, 128, span), lambda r, b, s: (r + first, b, 0, 0)),
        pl.BlockSpec((1, 1, span, 128), lambda r, b, s: (r + first, b, 0, 0)),
    ]
    args = [sc, x, dt, rate2, skip2, bt, c]
    body = functools.partial(scan_kernel, hb=hb, first=first)
    aliases = {}
    if out is not None:
        in_specs.append(pl.BlockSpec(memory_space=pl.ANY))
        aliases = {len(args): 0}
        args.append(out)
        inner = body

        def body(*refs):
            return inner(*refs[:7], *refs[8:])

    return pl.pallas_call(
        body,
        grid_spec=pltpu.PrefetchScalarGridSpec(
            num_scalar_prefetch=1,
            grid=(count, blocks),
            in_specs=in_specs,
            out_specs=x_spec,
            scratch_shapes=[
                pltpu.VMEM((16 * hb, 16 * hb), BF16),
                pltpu.VMEM((16 * hb, 16 * hb), BF16),
                pltpu.VMEM((BLOCK, BLOCK), BF16),
                pltpu.VMEM((hb, BLOCK, 128), BF16),
                pltpu.VMEM((hb, BLOCK, 128), BF16),
                pltpu.VMEM((hb, 128, 128), F32),
                pltpu.VMEM((8, 128), F32),
            ],
        ),
        out_shape=jax.ShapeDtypeStruct(x.shape, BF16),
        input_output_aliases=aliases,
        compiler_params=pltpu.CompilerParams(vmem_limit_bytes=40 << 20),
        cost_estimate=pl.CostEstimate(
            flops=count * heads * 16 * span * 128 * 128,
            bytes_accessed=count * heads * span * 512,
            transcendentals=count * heads * span * 128,
        ),
        name="span_scan",
    )(*args)


def page_kernel(sc, table_ref, kv_ref, *refs, dec_reqs, rows):
    count = len(refs) // 2
    head, row0 = sc[0], sc[3]
    reqs, _, pages = kv_ref.shape[:3]
    width = pages * PAGE_TOKENS
    lane = lax.broadcasted_iota(jnp.int32, (1, width), 1)
    for m in range(count):
        q_ref, out_ref = refs[m], refs[count + m]
        split, sub = sc[4 + reqs + 2 * m], sc[5 + reqs + 2 * m]
        kv_local = q_ref.shape[1]
        for i in range(dec_reqs):
            r = sub * dec_reqs + i
            place = jnp.zeros((1, width), jnp.int32)
            for p in range(pages):
                at = table_ref[row0 + r, head * pages + p] * PAGE_TOKENS - p * PAGE_TOKENS
                place = jnp.where(lane // PAGE_TOKENS == p, lane + at, place)
            valid = place < sc[4 + r]
            for v in range(kv_local):
                kv = kv_ref[r, split * kv_local + v]
                keys = kv[:, 0].reshape(width, HEAD_SIZE)
                values = kv[:, 1].reshape(width, HEAD_SIZE)
                s = dot_nt(q_ref[i, v], keys) * (1.0 / HEAD_SIZE**0.5)
                s = jnp.where(valid, s, NEG)
                top = jnp.max(s, axis=1, keepdims=True)
                w = jnp.where(valid, jnp.exp(s - top), 0.0)
                total = jnp.sum(w, axis=1, keepdims=True)
                high, low = split2(w)
                acc = dot(high, values) + dot(low, values)
                out_ref[i, v, 0:rows] = acc / jnp.maximum(total, 1e-30)
                lse = jnp.where(total > 0, top + jnp.log(jnp.maximum(total, 1e-30)), NEG)
                lse_t = jnp.broadcast_to(lse, (rows, HEAD_SIZE)).T[0:8]
                out_ref[i, v, rows:] = jnp.concatenate(
                    [lse_t, jnp.zeros((8, HEAD_SIZE - rows), F32)], axis=1
                )


def page_partials(sc, table, kv, queries, dec_reqs):
    rows = queries[0].shape[2]
    shape = queries[0].shape[:2] + (rows + 8, HEAD_SIZE)
    vmem = pl.BlockSpec(memory_space=pltpu.VMEM)
    return pl.pallas_call(
        functools.partial(page_kernel, dec_reqs=dec_reqs, rows=rows),
        in_specs=[pl.BlockSpec(memory_space=pltpu.SMEM)] * 2 + [vmem] * (1 + len(queries)),
        out_specs=[vmem] * len(queries),
        out_shape=[jax.ShapeDtypeStruct(shape, F32)] * len(queries),
        compiler_params=pltpu.CompilerParams(vmem_limit_bytes=40 << 20),
        cost_estimate=pl.CostEstimate(flops=10**9, bytes_accessed=6 << 20, transcendentals=10**6),
        name="page_partials",
    )(sc, table, kv, *queries)


def merge_kernel(q_ref, kn_ref, *refs, steps):
    parts, out_ref = refs[:-1], refs[-1]
    reqs, kv_local, rows, _ = q_ref.shape
    per_step = rows // steps
    step = lax.broadcasted_iota(jnp.int32, (rows, 1), 0) // per_step
    for r in range(reqs):
        for v in range(kv_local):
            q = q_ref[r, v].astype(F32)
            s = []
            for u in range(steps):
                key = kn_ref[r, v, 0, u : u + 1].astype(F32)
                one = jnp.sum(q * key, axis=1, keepdims=True) * (1.0 / HEAD_SIZE**0.5)
                s.append(jnp.where(step >= u, one, NEG))
            levels = []
            for part in parts:
                lse = part[r, v, rows:]
                levels.append(
                    jnp.concatenate([lse] * (HEAD_SIZE // 8), axis=0).T[0:rows, 0:1]
                )
            top = functools.reduce(jnp.maximum, s + levels)
            total = jnp.zeros((rows, 1), F32)
            acc = jnp.zeros((rows, HEAD_SIZE), F32)
            for u in range(steps):
                w = jnp.where(step >= u, jnp.exp(s[u] - top), 0.0)
                total = total + w
                acc = acc + w * kn_ref[r, v, 1, u : u + 1].astype(F32)
            for part, level in zip(parts, levels):
                w = jnp.exp(level - top)
                total = total + w
                acc = acc + w * part[r, v, 0:rows]
            out_ref[r, v] = (acc / total).astype(BF16)


def merge_partials(q, kv_new, parts, steps):
    vmem = pl.BlockSpec(memory_space=pltpu.VMEM)
    return pl.pallas_call(
        functools.partial(merge_kernel, steps=steps),
        in_specs=[vmem] * (2 + len(parts)),
        out_specs=vmem,
        out_shape=jax.ShapeDtypeStruct(q.shape, BF16),
        compiler_params=pltpu.CompilerParams(vmem_limit_bytes=40 << 20),
        cost_estimate=pl.CostEstimate(flops=10**8, bytes_accessed=2 << 20, transcendentals=10**5),
        name="merge_partials",
    )(q, kv_new, *parts)


def decode_kernel(sc, x_ref, dt_ref, rate_ref, skip_ref, b_ref, c_ref, *refs, count, part):
    messages, (state_ref, out_ref) = refs[:count], refs[-2:]
    split, group_heads = sc[0], H // G
    steps = x_ref.shape[1]
    blocks = x_ref.shape[2]
    b_all = b_ref[0].astype(F32)
    c_all = c_ref[0].astype(F32)
    which = lax.broadcasted_iota(jnp.int32, b_all.shape, 1)
    for m in range(count):
        z = sc[1 + m]
        group = ((z * sc[1 + count] + split) * part) // group_heads
        b = jnp.sum(jnp.where(which == group, b_all, 0.0), axis=1)
        c = jnp.sum(jnp.where(which == group, c_all, 0.0), axis=1)
        pad = jnp.zeros((8 - steps, 128), F32)
        b8 = jnp.concatenate([b, pad], axis=0)
        c8 = jnp.concatenate([c, pad], axis=0)
        gram = dot_nt(c8.astype(BF16), b8.astype(BF16))
        b_t = jnp.concatenate([b8] * 16, axis=0).T
        c16 = jnp.concatenate([c8, pad, c], axis=0)[0:8].astype(BF16)
        cc = jnp.concatenate([c16, c16], axis=1)
        rate = rate_ref[z, split]
        skip = skip_ref[z, split]
        dt = dt_ref[0, z]
        xs = [x_ref[0, j, z].astype(F32) for j in range(steps)]
        cum = []
        for j in range(steps):
            now = -rate * dt[:, j : j + 1]
            cum.append(now if j == 0 else cum[-1] + now)
        fed = [
            jnp.exp(cum[steps - 1] - cum[i]) * dt[:, i : i + 1] * xs[i] for i in range(steps)
        ]
        kept = jnp.broadcast_to(jnp.exp(cum[steps - 1]), (part, 128))
        message = messages[m]
        tops = message[0, part * 128 :, :].astype(F32)
        reads = []
        for h in range(part):
            code = message[0, h * 128 : (h + 1) * 128, :].astype(F32)
            size = (jnp.log2(jnp.abs(code)) + CODE / 2) * (tops[h : h + 1] * (1.0 / CODE))
            old = jnp.where(code < 0, -size, size)
            reads.append(dot(cc, jnp.concatenate(split2(old), axis=0)))
            new = old * kept[h : h + 1]
            for i in range(steps):
                new = new + b_t[:, i : i + 1] * fed[i][h : h + 1]
            state_ref[0, z, h] = new.T
        for j in range(steps):
            read = jnp.concatenate([one[j : j + 1] for one in reads], axis=0)
            out = jnp.exp(cum[j]) * read + skip * xs[j]
            for i in range(j + 1):
                out = out + (jnp.exp(cum[j] - cum[i]) * dt[:, i : i + 1] * gram[j : j + 1, i : i + 1]) * xs[i]
            out_ref[0, j, z] = out.astype(BF16)


def decode(sc, x, dt_t, rate4, skip4, b, c, messages, first, outs):
    reqs, steps, blocks, part, width = x.shape
    count = len(messages)
    step = messages[0].shape[0]
    per_req = lambda shape: pl.BlockSpec(
        (1,) + shape[1:], lambda r, s: (r + first,) + (0,) * (len(shape) - 1)
    )
    whole = lambda a: pl.BlockSpec(a.shape, lambda r, s: (0,) * a.ndim)
    in_specs = [per_req(x.shape), per_req(dt_t.shape), whole(rate4), whole(skip4), per_req(b.shape), per_req(c.shape)]
    in_specs += [pl.BlockSpec((1,) + m.shape[1:], lambda r, s: (r, 0, 0)) for m in messages]
    args = [sc, x, dt_t, rate4, skip4, b, c, *messages]
    aliases = {}
    if outs is not None:
        aliases = {len(args): 0, len(args) + 1: 1}
        in_specs += [pl.BlockSpec(memory_space=pl.ANY)] * 2
        args += list(outs)
    state_shape = (reqs, blocks, part, 128, 128)
    return pl.pallas_call(
        functools.partial(decode_kernel, count=count, part=part),
        grid_spec=pltpu.PrefetchScalarGridSpec(
            num_scalar_prefetch=1,
            grid=(step,),
            in_specs=in_specs,
            out_specs=[per_req(state_shape), per_req(x.shape)],
        ),
        out_shape=[jax.ShapeDtypeStruct(state_shape, F32), jax.ShapeDtypeStruct(x.shape, BF16)],
        input_output_aliases=aliases,
        compiler_params=pltpu.CompilerParams(vmem_limit_bytes=40 << 20),
        cost_estimate=pl.CostEstimate(
            flops=step * blocks * part * 128 * 128 * 16,
            bytes_accessed=step * blocks * part * 128 * 128 * 6,
            transcendentals=step * blocks * part * 128 * 128,
        ),
        name="decode_steps",
    )(*args)


def local(
    x_pre,
    dt_pre,
    b_pre,
    c_pre,
    rate,
    skip,
    lengths,
    table,
    kv_pages,
    query,
    kv_new,
    x_dec,
    dt_dec,
    b_dec,
    c_dec,
):
    n_head, n_req, n_pd = (lax.axis_size(a) for a in AXES)
    n_split = n_req * n_pd
    ratio = n_head // n_split
    head, req, pd = (lax.axis_index(a) for a in AXES)
    split = req * n_pd + pd
    reqs, span, heads, _ = x_pre.shape
    part = heads // n_split
    dec_reqs, steps, kv_local, query_width = query.shape
    hb = min(heads, H // G)
    blocks = heads // hb
    head_x, head_c, head_q = head // (n_pd * ratio), (head // ratio) % n_pd, head % ratio
    xor = jnp.bitwise_xor

    def index(h, x, c):
        return (h * n_req + x) * n_pd + c

    def places():
        return [(h, x, c) for h in range(n_head) for x in range(n_req) for c in range(n_pd)]

    groups = max(heads // (H // G), 1)
    group0 = (head * heads) // (H // G)
    b_own = lax.dynamic_slice_in_dim(b_pre, group0, groups, 2)
    c_own = lax.dynamic_slice_in_dim(c_pre, group0, groups, 2)
    bt = jnp.transpose(b_own, (0, 2, 3, 1))
    ct = jnp.transpose(c_own, (0, 2, 1, 3))
    rate2, skip2 = rate.reshape(n_head, heads), skip.reshape(n_head, heads)
    row0 = split * reqs
    own = lax.dynamic_slice_in_dim(lengths, row0, reqs, 0)

    def scalars(block, extra=()):
        first = jnp.stack([head, block, head_c, row0]).astype(jnp.int32)
        more = [jnp.stack(extra).astype(jnp.int32)] if extra else []
        return jnp.concatenate([first, own] + more)

    group_q = query_width // HEAD_SIZE
    q = query.reshape(dec_reqs, steps, kv_local, group_q, HEAD_SIZE)
    q = jnp.transpose(q, (0, 2, 1, 3, 4)).reshape(dec_reqs, kv_local, steps * group_q, HEAD_SIZE)
    sent, origin, routes = [], [], []
    for k in range(n_split):
        for i in range(ratio):
            route = []
            for h, x, c in places():
                to_split = h // ratio
                to_head = ((x * n_pd + c) ^ k) * ratio + ((h % ratio) ^ i)
                route.append((index(h, x, c), index(to_head, to_split // n_pd, to_split % n_pd)))
            sent.append(lax.ppermute(q, AXES, route))
            origin += [xor(head // ratio, k), xor(head % ratio, i)]
            routes.append([(b, a) for a, b in route])

    chunks = dec_reqs if ratio == 1 else 1
    size = reqs // chunks
    per_plane = heads // n_req
    mixed = []
    own_parts = []
    for chunk in range(chunks):
        if per_plane == hb:
            parts = [
                span_states(scalars(xor(req, j)), x_pre, dt_pre, rate2, bt, hb, part, chunk * size, size)
                for j in reversed(range(n_req))
            ][::-1]
        else:
            whole = span_states(scalars(jnp.int32(0)), x_pre, dt_pre, rate2, bt, hb, part, chunk * size, size)
            parts = [lax.dynamic_slice_in_dim(whole, xor(req, j) * n_pd, n_pd, 1) for j in range(n_req)]
        arrived = [parts[0]]
        for j in range(1, n_req):
            route = [(index(h, x, c), index(h, x ^ j, c)) for h, x, c in places()]
            arrived.append(lax.ppermute(parts[j], AXES, route))
        mixed.append(arrived)

    page_sums = page_partials(scalars(jnp.int32(0), origin), table, kv_pages, sent, dec_reqs)
    returned = [lax.ppermute(a, AXES, route) for a, route in zip(page_sums, routes)]

    rate4 = rate.reshape(n_head, n_split, part, 1)
    skip4 = skip.reshape(n_head, n_split, part, 1)
    dt_t = jnp.transpose(dt_dec, (0, 2, 3, 1))
    outs = None
    prefill = None
    for chunk in range(chunks):
        messages, sources = [], []
        for kj in range(n_req):
            from_x = xor(xor(head_x, req), kj)
            payload = mixed[chunk][0]
            for j in range(1, n_req):
                payload = jnp.where(from_x == j, mixed[chunk][j], payload)
            for kc in range(n_pd):
                for ki in range(ratio):
                    route = []
                    for h, x, c in places():
                        hx, hc, hq = h // (n_pd * ratio), (h // ratio) % n_pd, h % ratio
                        to = ((hx ^ kj) * n_pd + c) * ratio + (hq ^ ki)
                        route.append((index(h, x, c), index(to, x, hc ^ kc)))
                    piece = lax.dynamic_slice_in_dim(
                        payload[:, kc], xor(head_q, ki) * (size // ratio), size // ratio, 0
                    )
                    messages.append(lax.ppermute(piece, AXES, route))
                    sources.append((xor(head_x, kj) * n_pd + xor(pd, kc)) * ratio + xor(head_q, ki))
        sc = jnp.stack([split] + sources + [jnp.int32(n_split)]).astype(jnp.int32)
        prefill = span_scan(scalars(jnp.int32(0)), x_pre, dt_pre, rate2, skip2, bt, ct, hb, chunk * size, size, prefill)
        outs = decode(sc, x_dec, dt_t, rate4, skip4, b_dec, c_dec, messages, chunk * (dec_reqs // chunks), outs)
    decode_state, decode_out = outs

    news = jnp.transpose(kv_new, (0, 2, 3, 1, 4))
    attn = merge_partials(q, news, returned, steps)
    attn = attn.reshape(dec_reqs, kv_local, steps, group_q, HEAD_SIZE)
    attn_out = jnp.transpose(attn, (0, 2, 1, 3, 4)).reshape(query.shape)
    return (prefill, decode_out, decode_state, attn_out)


def solution(mesh):
    placed = (
        P(("group", "req", "pd"), None, "head", None),
        P(("group", "req", "pd"), None, "head"),
        P(("group", "req", "pd"), None, None, None),
        P(("group", "req", "pd"), None, None, None),
        P(),
        P(),
        P("group"),
        P("group", None),
        P(("group", "req", "pd"), None, "head", None, None, None),
        P(("group", "head"), None, ("req", "pd"), None),
        P(("group", "head"), None, ("req", "pd"), None, None),
        P(("group", "head"), None, None, ("req", "pd"), None),
        P(("group", "head"), None, None, ("req", "pd")),
        P(("group", "head"), None, None, None),
        P(("group", "head"), None, None, None),
    )
    return jax.shard_map(
        local,
        mesh=mesh,
        in_specs=placed,
        out_specs=(
            P(("group", "req", "pd"), None, "head", None),
            P(("group", "head"), None, None, ("req", "pd"), None),
            P(("group", "head"), None, ("req", "pd"), None, None),
            P(("group", "head"), None, ("req", "pd"), None),
        ),
        check_vma=False,
    )
```

```python
import functools

import jax
import jax.numpy as jnp
from jax import lax
from jax.experimental import pallas as pl
from jax.experimental.pallas import tpu as pltpu
from jax.sharding import PartitionSpec as P

H = 128
G = 8
HEAD_SIZE = 128
BLOCK = 128
PAGE_TOKENS = 32
NEG = -1e30
F32 = jnp.float32
BF16 = jnp.bfloat16
AXES = ("head", "req", "pd")
CODE = 240.0
PAD_ROWS = 16
VMEM = 40 << 20
LIGHT = pl.CostEstimate(flops=1, bytes_accessed=1, transcendentals=0)


def dot(a, b):
    return jnp.dot(a, b, preferred_element_type=F32)


def dot_nt(a, b):
    return lax.dot_general(a, b, (((1,), (1,)), ((), ())), preferred_element_type=F32)


def split2(v):
    high = v.astype(BF16)
    return high, (v - high.astype(F32)).astype(BF16)


def split3(v):
    high = v.astype(BF16)
    rest = v - high.astype(F32)
    middle = rest.astype(BF16)
    return high, middle, (rest - middle.astype(F32)).astype(BF16)


def swap_matrix(rows, cols):
    n = rows * cols
    i = lax.broadcasted_iota(jnp.int32, (n, n), 0)
    j = lax.broadcasted_iota(jnp.int32, (n, n), 1)
    return ((i // rows == j % cols) & (i % rows == j // cols)).astype(F32).astype(BF16)


def token_mask(shape, dim, length, start=0):
    return lax.broadcasted_iota(jnp.int32, shape, dim) + start < length


def scan_kernel(sc, skip_ref, x_hbm, b_hbm, c_hbm, dt_hbm, rate_ref, *refs, hb, part, first, reqs, heads):
    out_hbm, message_ref, x_buf, b_buf, c_buf, out_buf, blank = refs[-17:-10]
    perm, tri, select, rates_ref, dt_ref, xs, os, state, fetched, stored = refs[-10:]
    step = pl.program_id(0)
    r = sc[4 + reqs + first + step]
    head, block, flip = sc[0], sc[1], sc[2]
    length = sc[4 + r]
    span = dt_ref.shape[1]
    pairs = hb // 2
    chunks = span // BLOCK
    used = lax.shift_right_logical(length + (BLOCK - 1), BLOCK.bit_length() - 1)
    head0 = head * heads + block * hb
    group = lax.shift_right_logical(head0, (H // G).bit_length() - 1)
    h0 = pl.multiple_of(block * hb, hb)

    class fetch:
        def __init__(self, k):
            rows = pl.ds(pl.multiple_of(k * BLOCK, BLOCK), BLOCK)
            self.copies = [
                pltpu.make_async_copy(b_hbm.at[r, rows], b_buf.at[k], fetched.at[0, k]),
                pltpu.make_async_copy(c_hbm.at[r, rows], c_buf.at[k], fetched.at[1, k]),
                pltpu.make_async_copy(x_hbm.at[r, rows, pl.ds(h0, hb), :], x_buf.at[k], fetched.at[2, k]),
            ]

        def start(self):
            for copy in self.copies:
                copy.start()

        def wait(self):
            for copy in self.copies:
                copy.wait()

    def store(k, source):
        rows = pl.ds(pl.multiple_of(k * BLOCK, BLOCK), BLOCK)
        return pltpu.make_async_copy(source, out_hbm.at[r, rows, pl.ds(h0, hb), :], stored.at[k])

    steps = pltpu.make_async_copy(dt_hbm.at[r, pl.ds(h0, hb), :], dt_ref, stored.at[chunks])
    steps.start()
    for k in range(min(2, chunks)):

        @pl.when(k < used)
        def _():
            fetch(k).start()

    @pl.when(step == 0)
    def _():
        perm[...] = swap_matrix(16, hb)
        i = lax.broadcasted_iota(jnp.int32, (BLOCK, BLOCK), 0)
        j = lax.broadcasted_iota(jnp.int32, (BLOCK, BLOCK), 1)
        tri[...] = (i >= j).astype(F32).astype(BF16)
        i = lax.broadcasted_iota(jnp.int32, select.shape, 0)
        j = lax.broadcasted_iota(jnp.int32, select.shape, 1)
        select[...] = (j == i * G + group).astype(F32).astype(BF16)
        rates_ref[...] = jnp.broadcast_to(-rate_ref[...], (8, H)).T
        xs[...] = jnp.zeros(xs.shape, BF16)
        blank[...] = jnp.zeros(blank.shape, BF16)

    for k in range(chunks):

        @pl.when(k >= used)
        def _():
            store(k, blank).start()

    rates = rates_ref[pl.ds(pl.multiple_of(head0, hb), hb), 0:1]

    def chunk(k, fresh):
        lo = pl.multiple_of(k * BLOCK, BLOCK)
        valid = token_mask((hb, BLOCK), 1, length, lo)
        dt = dt_ref[:, pl.ds(lo, BLOCK)]
        dtm = jnp.where(valid, dt, 0.0)
        cum_t = sum(dot_nt(p, tri[...]) for p in split3(rates * dtm)[::-1])
        level_t = cum_t - jnp.where(valid, jnp.log(dt), NEG)
        last = cum_t[:, BLOCK - 1 : BLOCK]
        tail = jnp.exp(last - level_t)
        kept = jnp.exp(last)
        cum = cum_t.T
        grown = jnp.exp(cum)
        fetch(k).wait()

        @pl.when(k + 2 < used)
        def _():
            fetch(k + 2).start()

        both = []
        for t in range(0, BLOCK, 256 // G):
            rows = slice(t, t + 256 // G)
            tiles = [ref[k, rows].reshape(256, 128) for ref in (b_buf, c_buf)]
            both.append(dot(select[...], jnp.concatenate(tiles, axis=1)))
        both = jnp.concatenate(both, axis=0)
        bt = both[:, 0:128].T
        c = both[:, 128:].astype(BF16)
        cc = jnp.concatenate([c, c], axis=1)
        scores = dot(c, bt.astype(BF16)) * tri[...].astype(F32)
        for t in range(0, BLOCK, 32):
            tiles = [x_buf[k, t + u : t + u + 16].reshape(16 * hb, 128) for u in (0, 16)]
            y = dot(perm[...], jnp.concatenate(tiles, axis=1)).astype(BF16)
            for h in range(hb):
                a, i = divmod(h, 2)
                for u in range(2):
                    xs[a, i * 128 + t + u * 16 : i * 128 + t + u * 16 + 16, i * 128 : (i + 1) * 128] = y[
                        h * 16 : (h + 1) * 16, u * 128 : (u + 1) * 128
                    ]

        for a in range(pairs):
            split_w, split_t = [], []
            for h in (2 * a, 2 * a + 1):
                diff = cum[:, h : h + 1] - level_t[h : h + 1, :]
                split_w.append(split2(jnp.exp(jnp.minimum(diff, 80.0)) * scores))
                split_t.append(split2(bt * tail[h : h + 1]))
            left = jnp.concatenate(
                [
                    jnp.concatenate([s[i][j] for j in range(2) for i in range(2)], axis=1)
                    for s in (split_w, split_t)
                ],
                axis=0,
            )
            x = xs[a]
            both = dot(left[:, :256], x) + dot(left[:, 256:], x)
            wide = lambda f: jnp.concatenate([f(0), f(1)], axis=1)
            out = both[:BLOCK] + wide(
                lambda i: skip_ref[head0 + 2 * a + i]
                * x[i * 128 : (i + 1) * 128, i * 128 : (i + 1) * 128].astype(F32)
            )
            new = both[BLOCK:]
            if not fresh:
                old = state[a]
                inter = dot(cc, jnp.concatenate(split2(old), axis=0))
                out = out + wide(
                    lambda i: grown[:, 2 * a + i : 2 * a + i + 1] * inter[:, i * 128 : (i + 1) * 128]
                )
                new = new + wide(
                    lambda i: kept[2 * a + i : 2 * a + i + 1, :] * old[:, i * 128 : (i + 1) * 128]
                )
            state[a] = new
            out = out.astype(BF16)
            os[2 * a] = out[:, :128]
            os[2 * a + 1] = out[:, 128:]
        out_buf[k] = jnp.swapaxes(os[...], 0, 1)

        @pl.when(lo + BLOCK > length)
        def _():
            out = out_buf[k]
            keep = lax.broadcasted_iota(jnp.int32, out.shape, 0) + lo < length
            out_buf[k] = jnp.where(keep, out.astype(F32), 0.0).astype(BF16)

        store(k, out_buf.at[k]).start()

    steps.wait()
    chunk(0, True)

    @pl.loop(1, used)
    def _(k):
        chunk(k, False)

    for p in range(hb // part):
        slot = jnp.bitwise_xor(p, flip)
        tops = []
        for i in range(part):
            h = p * part + i
            st = state[h // 2, :, (h % 2) * 128 : (h % 2) * 128 + 128]
            size = jnp.abs(st)
            top = (jnp.max(size, axis=0, keepdims=True) * 1.01 + 1e-30).astype(BF16).astype(F32)
            code = jnp.exp2(size * (CODE / top) - CODE / 2)
            message_ref[slot, 0, i * 128 : (i + 1) * 128, :] = jnp.where(st < 0, -code, code).astype(BF16)
            tops.append(top)
        tops.append(jnp.zeros((PAD_ROWS - part, 128), F32))
        message_ref[slot, 0, part * 128 :, :] = jnp.concatenate(tops, axis=0).astype(BF16)
    for k in range(chunks):
        store(k, blank).wait()


def span_scan(sc, x, b, c, dt_t, rate, skip, hb, part, first, count, out):
    reqs, span, heads, width = x.shape
    chunks = span // BLOCK
    slots, rows = hb // part, part * 128 + PAD_ROWS
    in_specs = [
        pl.BlockSpec(memory_space=pltpu.SMEM),
        pl.BlockSpec(memory_space=pltpu.HBM),
        pl.BlockSpec(memory_space=pltpu.HBM),
        pl.BlockSpec(memory_space=pltpu.HBM),
        pl.BlockSpec(memory_space=pltpu.HBM),
        pl.BlockSpec((1, H), lambda r, s: (0, 0)),
    ]
    args = [sc, skip, x, b, c, dt_t, rate.reshape(1, H)]
    aliases = {}
    if out is not None:
        in_specs.append(pl.BlockSpec(memory_space=pltpu.HBM))
        aliases = {len(args): 0}
        args.append(out)
    block = (BLOCK, hb, width)
    return pl.pallas_call(
        functools.partial(scan_kernel, hb=hb, part=part, first=first, reqs=reqs, heads=heads),
        grid_spec=pltpu.PrefetchScalarGridSpec(
            num_scalar_prefetch=1,
            grid=(count,),
            in_specs=in_specs,
            out_specs=[
                pl.BlockSpec(memory_space=pltpu.HBM),
                pl.BlockSpec((slots, 1, rows, 128), lambda r, s: (0, r, 0, 0)),
            ],
            scratch_shapes=[
                pltpu.VMEM((chunks,) + block, BF16),
                pltpu.VMEM((chunks, BLOCK) + b.shape[2:], BF16),
                pltpu.VMEM((chunks, BLOCK) + c.shape[2:], BF16),
                pltpu.VMEM((chunks,) + block, BF16),
                pltpu.VMEM(block, BF16),
                pltpu.VMEM((16 * hb, 16 * hb), BF16),
                pltpu.VMEM((BLOCK, BLOCK), BF16),
                pltpu.VMEM((256 // G, 256), BF16),
                pltpu.VMEM((H, 8), F32),
                pltpu.VMEM((hb, span), F32),
                pltpu.VMEM((hb // 2, 256, 256), BF16),
                pltpu.VMEM((hb, BLOCK, 128), BF16),
                pltpu.VMEM((hb // 2, 128, 256), F32),
                pltpu.SemaphoreType.DMA((3, chunks)),
                pltpu.SemaphoreType.DMA((chunks + 1,)),
            ],
        ),
        out_shape=[
            jax.ShapeDtypeStruct(x.shape, BF16),
            jax.ShapeDtypeStruct((slots, count, rows, 128), BF16),
        ],
        input_output_aliases=aliases,
        compiler_params=pltpu.CompilerParams(vmem_limit_bytes=61 << 20),
        cost_estimate=LIGHT,
        name="span_scan",
    )(*args)


def page_kernel(sc, table_ref, kv_ref, q_ref, out_ref, *, rows):
    count, dec_reqs, kv_local = q_ref.shape[:3]
    head, row0 = sc[0], sc[3]
    reqs, _, pages = kv_ref.shape[:3]
    width = pages * PAGE_TOKENS
    lane = lax.broadcasted_iota(jnp.int32, (1, width), 1)
    for r in range(reqs):
        place = jnp.zeros((1, width), jnp.int32)
        for p in range(pages):
            at = table_ref[row0 + r, head * pages + p] * PAGE_TOKENS - p * PAGE_TOKENS
            place = jnp.where(lane // PAGE_TOKENS == p, lane + at, place)
        valid = place < sc[4 + r]
        for m in range(count):
            if m % (reqs // dec_reqs) != r // dec_reqs:
                continue
            i = r % dec_reqs
            for v in range(kv_local):
                kv = kv_ref[r, (m // (reqs // dec_reqs)) * kv_local + v]
                keys = kv[:, 0].reshape(width, HEAD_SIZE)
                values = kv[:, 1].reshape(width, HEAD_SIZE)
                s = dot_nt(q_ref[m, i, v, 0:rows], keys) * (1.0 / HEAD_SIZE**0.5)
                s = jnp.where(valid, s, NEG)
                top = jnp.max(s, axis=1, keepdims=True)
                w = jnp.where(valid, jnp.exp(s - top), 0.0)
                total = jnp.sum(w, axis=1, keepdims=True)
                high, low = split2(w)
                acc = dot(high, values) + dot(low, values)
                out_ref[m, i, v, 0:rows] = acc / jnp.maximum(total, 1e-30)
                lse = jnp.where(total > 0, top + jnp.log(jnp.maximum(total, 1e-30)), NEG)
                lse_t = jnp.broadcast_to(lse, (rows, HEAD_SIZE)).T[0:8]
                out_ref[m, i, v, rows:] = jnp.concatenate(
                    [lse_t, jnp.zeros((8, HEAD_SIZE - rows), F32)], axis=1
                )


def page_partials(sc, table, kv, q, rows):
    vmem = pl.BlockSpec(memory_space=pltpu.VMEM)
    return pl.pallas_call(
        functools.partial(page_kernel, rows=rows),
        in_specs=[pl.BlockSpec(memory_space=pltpu.SMEM)] * 2 + [vmem] * 2,
        out_specs=vmem,
        out_shape=jax.ShapeDtypeStruct(q.shape[:3] + (rows + 8, HEAD_SIZE), F32),
        compiler_params=pltpu.CompilerParams(vmem_limit_bytes=VMEM),
        cost_estimate=LIGHT,
        name="page_partials",
    )(sc, table, kv, q)


def merge_kernel(q_ref, parts_ref, out_ref, *, steps, rows):
    count, reqs, kv_local = parts_ref.shape[:3]
    per_step = rows // steps
    step = lax.broadcasted_iota(jnp.int32, (rows, 1), 0) // per_step
    for r in range(reqs):
        for v in range(kv_local):
            both = q_ref[r, v].astype(F32)
            q, news = both[0:rows], both[rows:]
            s = []
            for u in range(steps):
                one = jnp.sum(q * news[u : u + 1], axis=1, keepdims=True) * (1.0 / HEAD_SIZE**0.5)
                s.append(jnp.where(step >= u, one, NEG))
            levels = []
            for m in range(count):
                lse = parts_ref[m, r, v, rows:]
                levels.append(jnp.concatenate([lse] * (HEAD_SIZE // 8), axis=0).T[0:rows, 0:1])
            top = functools.reduce(jnp.maximum, s + levels)
            total = jnp.zeros((rows, 1), F32)
            acc = jnp.zeros((rows, HEAD_SIZE), F32)
            for u in range(steps):
                w = jnp.where(step >= u, jnp.exp(s[u] - top), 0.0)
                total = total + w
                acc = acc + w * news[steps + u : steps + u + 1]
            for m, level in enumerate(levels):
                w = jnp.exp(level - top)
                total = total + w
                acc = acc + w * parts_ref[m, r, v, 0:rows]
            out_ref[r, v] = (acc / total).astype(BF16)


def merge_partials(q, parts, steps, rows):
    vmem = pl.BlockSpec(memory_space=pltpu.VMEM)
    return pl.pallas_call(
        functools.partial(merge_kernel, steps=steps, rows=rows),
        in_specs=[vmem] * 2,
        out_specs=vmem,
        out_shape=jax.ShapeDtypeStruct(q.shape[:2] + (rows, HEAD_SIZE), BF16),
        compiler_params=pltpu.CompilerParams(vmem_limit_bytes=VMEM),
        cost_estimate=LIGHT,
        name="merge_partials",
    )(q, parts)


def decode_kernel(sc, x_ref, dt_ref, rate_ref, skip_ref, b_ref, c_ref, *refs, count, part):
    messages, (state_ref, out_ref) = refs[:count], refs[-2:]
    split, group_heads = sc[0], H // G
    steps = x_ref.shape[1]
    blocks = x_ref.shape[2]
    b_all = b_ref[0].astype(F32)
    c_all = c_ref[0].astype(F32)
    which = lax.broadcasted_iota(jnp.int32, b_all.shape, 1)
    for m in range(count):
        z = sc[1 + m]
        group = ((z * sc[1 + count] + split) * part) // group_heads
        b = jnp.sum(jnp.where(which == group, b_all, 0.0), axis=1)
        c = jnp.sum(jnp.where(which == group, c_all, 0.0), axis=1)
        pad = jnp.zeros((8 - steps, 128), F32)
        b8 = jnp.concatenate([b, pad], axis=0)
        c8 = jnp.concatenate([c, pad], axis=0)
        gram = dot_nt(c8.astype(BF16), b8.astype(BF16))
        b_t = jnp.concatenate([b8] * 16, axis=0).T
        c16 = jnp.concatenate([c8, pad, c], axis=0)[0:8].astype(BF16)
        cc = jnp.concatenate([c16, c16], axis=1)
        rate = rate_ref[z, split]
        skip = skip_ref[z, split]
        dt = dt_ref[0, z]
        xs = [x_ref[0, j, z].astype(F32) for j in range(steps)]
        cum = []
        for j in range(steps):
            now = -rate * dt[:, j : j + 1]
            cum.append(now if j == 0 else cum[-1] + now)
        fed = [
            jnp.exp(cum[steps - 1] - cum[i]) * dt[:, i : i + 1] * xs[i] for i in range(steps)
        ]
        kept = jnp.broadcast_to(jnp.exp(cum[steps - 1]), (part, 128))
        message = messages[m]
        tops = message[0, part * 128 :, :].astype(F32)
        reads = []
        for h in range(part):
            code = message[0, h * 128 : (h + 1) * 128, :].astype(F32)
            size = (jnp.log2(jnp.abs(code)) + CODE / 2) * (tops[h : h + 1] * (1.0 / CODE))
            old = jnp.where(code < 0, -size, size)
            reads.append(dot(cc, jnp.concatenate(split2(old), axis=0)))
            new = old * kept[h : h + 1]
            for i in range(steps):
                new = new + b_t[:, i : i + 1] * fed[i][h : h + 1]
            state_ref[0, z, h] = new.T
        for j in range(steps):
            read = jnp.concatenate([one[j : j + 1] for one in reads], axis=0)
            out = jnp.exp(cum[j]) * read + skip * xs[j]
            for i in range(j + 1):
                out = out + (jnp.exp(cum[j] - cum[i]) * dt[:, i : i + 1] * gram[j : j + 1, i : i + 1]) * xs[i]
            out_ref[0, j, z] = out.astype(BF16)


def decode(sc, x, dt_t, rate4, skip4, b, c, messages, first, outs):
    reqs, steps, blocks, part, width = x.shape
    count = len(messages)
    step = messages[0].shape[0]
    per_req = lambda shape: pl.BlockSpec(
        (1,) + shape[1:], lambda r, s: (s[2 + count + first + r],) + (0,) * (len(shape) - 1)
    )
    whole = lambda a: pl.BlockSpec(a.shape, lambda r, s: (0,) * a.ndim)
    in_specs = [per_req(x.shape), per_req(dt_t.shape), whole(rate4), whole(skip4), per_req(b.shape), per_req(c.shape)]
    in_specs += [pl.BlockSpec((1,) + m.shape[1:], lambda r, s: (r, 0, 0)) for m in messages]
    args = [sc, x, dt_t, rate4, skip4, b, c, *messages]
    aliases = {}
    if outs is not None:
        aliases = {len(args): 0, len(args) + 1: 1}
        in_specs += [pl.BlockSpec(memory_space=pltpu.HBM)] * 2
        args += list(outs)
    state_shape = (reqs, blocks, part, 128, 128)
    return pl.pallas_call(
        functools.partial(decode_kernel, count=count, part=part),
        grid_spec=pltpu.PrefetchScalarGridSpec(
            num_scalar_prefetch=1,
            grid=(step,),
            in_specs=in_specs,
            out_specs=[per_req(state_shape), per_req(x.shape)],
        ),
        out_shape=[jax.ShapeDtypeStruct(state_shape, F32), jax.ShapeDtypeStruct(x.shape, BF16)],
        input_output_aliases=aliases,
        compiler_params=pltpu.CompilerParams(vmem_limit_bytes=VMEM),
        cost_estimate=LIGHT,
        name="decode_steps",
    )(*args)


def local(
    x_pre,
    dt_pre,
    b_pre,
    c_pre,
    rate,
    skip,
    lengths,
    table,
    kv_pages,
    query,
    kv_new,
    x_dec,
    dt_dec,
    b_dec,
    c_dec,
):
    n_head, n_req, n_pd = (lax.axis_size(a) for a in AXES)
    n_split = n_req * n_pd
    ratio = n_head // n_split
    head, req, pd = (lax.axis_index(a) for a in AXES)
    split = req * n_pd + pd
    reqs, span, heads, _ = x_pre.shape
    part = heads // n_split
    dec_reqs, steps, kv_local, query_width = query.shape
    hb = min(heads, H // G)
    blocks = heads // hb
    head_x, head_c, head_q = head // (n_pd * ratio), (head // ratio) % n_pd, head % ratio
    xor = jnp.bitwise_xor

    def index(h, x, c):
        return (h * n_req + x) * n_pd + c

    def places():
        return [(h, x, c) for h in range(n_head) for x in range(n_req) for c in range(n_pd)]

    def after(value, *earlier):
        return lax.optimization_barrier((value,) + earlier)[0] if earlier else value

    sizes = [1] * reqs if ratio == 1 else [reqs]
    chunks = len(sizes)
    starts = [sum(sizes[:k]) for k in range(chunks)]
    per_plane = heads // n_req
    dt_t_pre = jnp.transpose(dt_pre, (0, 2, 1))
    row0 = split * reqs
    own = lax.dynamic_slice_in_dim(lengths, row0, reqs, 0)

    def ordered(values):
        if chunks == 1:
            return jnp.arange(values.shape[0], dtype=jnp.int32)
        at = jnp.arange(values.shape[0], dtype=jnp.int32)
        before = (values[None, :] < values[:, None]) | (
            (values[None, :] == values[:, None]) & (at[None, :] < at[:, None])
        )
        rank = jnp.sum(before.astype(jnp.int32), axis=1)
        return jnp.sum(jnp.where(rank[None, :] == at[:, None], at[None, :], 0), axis=1).astype(jnp.int32)

    order = ordered(own)

    def scalars(block):
        first = jnp.stack([head, block, head_c, row0]).astype(jnp.int32)
        return jnp.concatenate([first, own, order])

    prefill = None

    def scan(chunk, blocks, *earlier):
        nonlocal prefill
        found = []
        for block in blocks:
            prefill, message = span_scan(
                after(scalars(block), *earlier), x_pre, b_pre, c_pre, dt_t_pre, rate, skip, hb, part, starts[chunk], sizes[chunk], prefill
            )
            found.append(message)
        return found

    def to_planes(parts):
        routes = [[(index(h, x, c), index(h, x ^ j, c)) for h, x, c in places()] for j in range(1, n_req)]
        return [lax.ppermute(p, AXES, route) for p, route in zip(parts, routes)]

    def payloads(arrived):
        out = []
        for kj in range(n_req):
            from_x = xor(xor(head_x, req), kj)
            payload = arrived[0]
            for j in range(1, n_req):
                payload = jnp.where(from_x == j, arrived[j], payload)
            for kc in range(n_pd):
                for ki in range(ratio):
                    out.append(
                        lax.dynamic_slice_in_dim(
                            payload[kc], xor(head_q, ki) * (payload.shape[1] // ratio), payload.shape[1] // ratio, 0
                        )
                    )
        return out

    def along_heads(pieces):
        out = []
        for n, piece in enumerate(pieces):
            kj, kc, ki = n // (n_pd * ratio), (n // ratio) % n_pd, n % ratio
            route = []
            for h, x, c in places():
                hx, hc, hq = h // (n_pd * ratio), (h // ratio) % n_pd, h % ratio
                to = ((hx ^ kj) * n_pd + c) * ratio + (hq ^ ki)
                route.append((index(h, x, c), index(to, x, hc ^ kc)))
            out.append(lax.ppermute(piece, AXES, route))
        return out

    group_q = query_width // HEAD_SIZE
    rows = steps * group_q
    turn = []
    for h, x, c in places():
        to_split = h // ratio
        turn.append((index(h, x, c), index((x * n_pd + c) * ratio + h % ratio, to_split // n_pd, to_split % n_pd)))
    q = query.reshape(dec_reqs, steps, kv_local, group_q, HEAD_SIZE)
    q = jnp.transpose(q, (0, 2, 1, 3, 4)).reshape(dec_reqs, kv_local, rows, HEAD_SIZE)
    news = jnp.transpose(kv_new, (0, 2, 3, 1, 4)).reshape(dec_reqs, kv_local, 2 * steps, HEAD_SIZE)
    turned = lax.ppermute(jnp.concatenate([q, news], axis=2), AXES, turn)

    def attention(before_queries, before_pages):
        copies = jnp.broadcast_to(after(turned, *before_queries)[None], (n_head,) + turned.shape)
        shared = lax.all_to_all(copies, "head", split_axis=0, concat_axis=0, tiled=True)
        sums = page_partials(after(scalars(jnp.int32(0)), *before_pages), table, kv_pages, shared, rows)
        return sums, lax.all_to_all(sums, "head", split_axis=0, concat_axis=0, tiled=True)

    messages, pieces = [], []
    for chunk in range(chunks):
        if per_plane == hb:
            others = scan(chunk, [xor(req, j) for j in range(1, n_req)], *(messages[chunk - 3] if chunk > 2 else ()))
            moved = to_planes(others)
            if chunk:
                messages.append(along_heads(pieces))
            own_part = scan(chunk, [req], *pieces, *(messages[chunk - 2] if chunk > 2 else ()))
        else:
            whole = scan(chunk, [jnp.int32(0)])[0]
            parts = [lax.dynamic_slice_in_dim(whole, xor(req, j) * n_pd, n_pd, 0) for j in range(n_req)]
            moved = to_planes(parts[1:])
            own_part = parts[:1]
        pieces = payloads(own_part + moved)
        if chunk == 0:
            first_pieces = pieces
        if chunk == min(2, chunks - 1):
            sums, partials = attention(first_pieces, own_part)

    rate4 = rate.reshape(n_head, n_split, part, 1)
    skip4 = skip.reshape(n_head, n_split, part, 1)
    dt_t = jnp.transpose(dt_dec, (0, 2, 3, 1))
    sources = [
        (xor(head_x, kj) * n_pd + xor(pd, kc)) * ratio + xor(head_q, ki)
        for kj in range(n_req)
        for kc in range(n_pd)
        for ki in range(ratio)
    ]
    dec_order = ordered(lax.dynamic_slice_in_dim(lengths, head * dec_reqs, dec_reqs, 0))
    sc = jnp.concatenate([jnp.stack([split] + sources + [jnp.int32(n_split)]).astype(jnp.int32), dec_order])
    outs = None

    def decode_chunk(chunk, *earlier):
        return decode(
            after(sc, *earlier), x_dec, dt_t, rate4, skip4, b_dec, c_dec, messages[chunk], starts[chunk], outs
        )

    early = max(chunks - 2, 0)
    for chunk in range(early):
        outs = decode_chunk(chunk, *pieces)
    if early:
        pieces = [after(piece, *outs) for piece in pieces]
    messages.append(along_heads(pieces))
    for chunk in range(early, chunks):
        outs = decode_chunk(chunk)
    decode_state, decode_out = outs

    attn = merge_partials(turned, partials, steps, rows)
    attn = lax.ppermute(attn, AXES, [(b, a) for a, b in turn])
    attn = attn.reshape(dec_reqs, kv_local, steps, group_q, HEAD_SIZE)
    attn_out = jnp.transpose(attn, (0, 2, 1, 3, 4)).reshape(query.shape)
    return (prefill, decode_out, decode_state, attn_out)


def solution(mesh):
    placed = (
        P(("group", "req", "pd"), None, "head", None),
        P(("group", "req", "pd"), None, "head"),
        P(("group", "req", "pd"), None, None, None),
        P(("group", "req", "pd"), None, None, None),
        P(),
        P(),
        P("group"),
        P("group", None),
        P(("group", "req", "pd"), None, "head", None, None, None),
        P(("group", "head"), None, ("req", "pd"), None),
        P(("group", "head"), None, ("req", "pd"), None, None),
        P(("group", "head"), None, None, ("req", "pd"), None),
        P(("group", "head"), None, None, ("req", "pd")),
        P(("group", "head"), None, None, None),
        P(("group", "head"), None, None, None),
    )
    return jax.shard_map(
        local,
        mesh=mesh,
        in_specs=placed,
        out_specs=(
            P(("group", "req", "pd"), None, "head", None),
            P(("group", "head"), None, None, ("req", "pd"), None),
            P(("group", "head"), None, ("req", "pd"), None, None),
            P(("group", "head"), None, ("req", "pd"), None),
        ),
        check_vma=False,
    )
```
